32 devices in a mesh: sfc: 32 (over z, y, x, core).
Axes of the slice: x: 2, y: 2, z: 4, core: 2. Of those that a mesh axis runs over, the one named last changes fastest.
Arguments:
- state: float32 [5, 2048, 512], P(None, 'sfc'), may hold values from -0.47 to 4.3, as said below
- volume: int32 [2048, 512], P('sfc'), may hold values from 1 to 8, as said below
- neighbour: int32 [2048, 6], P('sfc'), may hold values from -1 to 2047, as said below
- parent: int32 [2048], P('sfc'), may hold values from 0 to 2047, as said below
Outputs:
- fine_state: float32 [5, 2048, 512], P(None, 'sfc')
- coarse_state: float32 [5, 256, 512], P(None, 'sfc')
- coarse_residual: float32 [5, 256, 512], P(None, 'sfc')
The draws below stay inside these ranges and needn't reach their ends.
Inputs may be any that keep to these rules, and one draw needn't show every extreme that they name: `state`: each cell has density 0.65 to 1.55, x velocity 0.2 to 0.8, y and z velocity of size 0.3 at most, pressure 0.55 to 1.45, and total energy = pressure / 0.4 + half the density times the squared speed. `volume`: every cell of a brick that is not cut holds 8; a cut brick has some cell under 8. One device's 64 bricks hold at most 16 cut bricks, and some device holds exactly 16. `neighbour`: the fine bricks form a grid of 16 x 16 x 8, periodic along y, with -1 on the far-field faces at the ends of x and z. The grid is cut into cubes of 4 x 4 x 4 bricks, ordered along a Morton curve: device d holds the cube whose coordinates (in cubes) have bit i // 3 of x, y or z equal to bit i of d, as i % 3 is 0, 1 or 2, as bricks d * 64 to (d + 1) * 64 - 1 in no particular order. The relation is symmetric. `parent`: every pair of a coarse brick and an octant occurs exactly once; the octant gives the parities of the fine brick's x, y and z positions. The coarse level is the fine grid halved, ordered along its own Morton curve and cut into runs of 8 that start half a run later than the fine level's cuts: coarse brick c is held by device c // 8, and of each device's fine bricks exactly 32 have their parents on the next device (the last device's on device 0) and the rest on the device itself.
All inputs are finite; a program needn't handle non-finite values.
Results may differ from the reference program's by a relative error of at most 0.00002.
Values sent between devices are 32-bit elements; how exact they have to be, the bound alone decides.
A program may use at most 128 MiB of HBM per device.

```python
import jax
import jax.numpy as jnp
from jax import lax

BE = 8
CUBE = 4
GX = 16
GY = 16
GZ = 8
BRICK_DEV = 64
BRICKS = 2048
CBRICK_DEV = 8
CUT_MAX = 16


def random_orders(key, rows_count, length):
    return jax.vmap(lambda sub_key: jax.random.permutation(sub_key, length))(jax.random.split(key, rows_count)).astype(jnp.int32)


def alternate(coords, bit_total):
    result = jnp.zeros_like(coords[0])
    for position in range(bit_total):
        level_index = position // 3
        result = result + coords[position % 3] // 2 ** level_index % 2 * 2 ** position
    return result


def layout_tables(key):
    device_total = BRICKS // BRICK_DEV
    device_bits = device_total.bit_length() - 1
    cube_bits = CUBE.bit_length() - 1
    fine_perm = random_orders(jax.random.fold_in(key, 101), device_total, BRICK_DEV)
    coarse_perm = random_orders(jax.random.fold_in(key, 202), device_total, CBRICK_DEV)
    grid_shape = (GX, GY, GZ)
    x_grid = jnp.broadcast_to(jnp.arange(GX, dtype=jnp.int32)[:, None, None], grid_shape)
    y_grid = jnp.broadcast_to(jnp.arange(GY, dtype=jnp.int32)[None, :, None], grid_shape)
    z_grid = jnp.broadcast_to(jnp.arange(GZ, dtype=jnp.int32)[None, None, :], grid_shape)
    device_id = alternate((x_grid // CUBE, y_grid // CUBE, z_grid // CUBE), device_bits)
    local_id = alternate((x_grid % CUBE, y_grid % CUBE, z_grid % CUBE), 3 * cube_bits)
    brick_id = device_id * BRICK_DEV + fine_perm[device_id, local_id]
    entries = [jnp.where(x_grid > 0, jnp.roll(brick_id, 1, axis=0), -1), jnp.where(x_grid < GX - 1, jnp.roll(brick_id, -1, axis=0), -1), jnp.roll(brick_id, 1, axis=1), jnp.roll(brick_id, -1, axis=1), jnp.where(z_grid > 0, jnp.roll(brick_id, 1, axis=2), -1), jnp.where(z_grid < GZ - 1, jnp.roll(brick_id, -1, axis=2), -1)]
    flat_ids = brick_id.reshape(-1)
    neighbour_table = jnp.zeros((BRICKS, 6), jnp.int32).at[flat_ids].set(jnp.stack(entries, axis=-1).reshape(-1, 6).astype(jnp.int32))
    half_cube = CUBE // 2
    coarse_local = alternate((x_grid // 2 % half_cube, y_grid // 2 % half_cube, z_grid // 2 % half_cube), 3 * (cube_bits - 1))
    curve_pos = device_id * CBRICK_DEV + coarse_local + CBRICK_DEV // 2
    owner_dev = curve_pos // CBRICK_DEV % device_total
    coarse_id = owner_dev * CBRICK_DEV + coarse_perm[owner_dev, curve_pos % CBRICK_DEV]
    octant = (x_grid % 2 * 2 + y_grid % 2) * 2 + z_grid % 2
    parent_table = jnp.zeros((BRICKS,), jnp.int32).at[flat_ids].set((coarse_id * 8 + octant).reshape(-1).astype(jnp.int32))
    return (neighbour_table, parent_table)


def draw_neighbour(key, part):
    return layout_tables(key)[0]


def draw_parent(key, part):
    return layout_tables(key)[1]


def draw_volume(key, part):
    device_total = BRICKS // BRICK_DEV
    count_key, top_key, order_key, level_key, first_key = jax.random.split(jax.random.fold_in(key, 303), 5)
    cut_counts = jax.random.randint(count_key, (device_total,), 0, CUT_MAX + 1)
    busiest = jax.random.randint(top_key, (), 0, device_total)
    cut_counts = cut_counts.at[busiest].set(CUT_MAX)
    orders = random_orders(order_key, device_total, BRICK_DEV)
    is_cut = orders < cut_counts[:, None]
    levels = jax.random.randint(level_key, (device_total, BRICK_DEV, BE ** 3), 1, 9)
    first_cell = jax.random.randint(first_key, (device_total, BRICK_DEV), 1, 8)
    levels = levels.at[:, :, 0].set(first_cell)
    return jnp.where(is_cut[:, :, None], levels, 8).astype(jnp.int32).reshape(BRICKS, BE ** 3)


def draw_state(key, part):
    key_list = jax.random.split(jax.random.fold_in(key, 404), 5)
    grid_shape = (BRICKS, BE ** 3)
    density = 1.1 + 0.15 * jnp.clip(jax.random.normal(key_list[0], grid_shape, jnp.float32), -3.0, 3.0)
    speed_x = 0.5 + 0.1 * jnp.clip(jax.random.normal(key_list[1], grid_shape, jnp.float32), -3.0, 3.0)
    speed_y = 0.1 * jnp.clip(jax.random.normal(key_list[2], grid_shape, jnp.float32), -3.0, 3.0)
    speed_z = 0.1 * jnp.clip(jax.random.normal(key_list[3], grid_shape, jnp.float32), -3.0, 3.0)
    pressure = 1.0 + 0.15 * jnp.clip(jax.random.normal(key_list[4], grid_shape, jnp.float32), -3.0, 3.0)
    energy = pressure / 0.4 + 0.5 * density * (speed_x * speed_x + speed_y * speed_y + speed_z * speed_z)
    return jnp.stack([density, density * speed_x, density * speed_y, density * speed_z, energy]).astype(jnp.float32)


def setup_inputs(seed: int = 0) -> dict:
    splits = jax.random.split(jax.random.key(seed), 5)
    state = draw_state(jax.random.fold_in(splits[4], 71), 0)
    volume = draw_volume(jax.random.fold_in(splits[4], 71), 0)
    neighbour = draw_neighbour(jax.random.fold_in(splits[4], 71), 0)
    parent = draw_parent(jax.random.fold_in(splits[4], 71), 0)
    return {"state": state, "volume": volume, "neighbour": neighbour, "parent": parent}


HEAT_RATIO = 1.4
CFL_NUMBER = 0.25
FIRST_SECTION = 0.5

def free_stream():
    energy = 1.0 / (HEAT_RATIO * (HEAT_RATIO - 1.0)) + 0.125
    return jnp.array([1.0, 0.5, 0.0, 0.0, energy], dtype=jnp.float32)

def one_side(conserved, direction):
    density = conserved[0]
    velocity = conserved[1 + direction] / density
    kinetic = 0.5 * (conserved[1] * conserved[1] + conserved[2] * conserved[2] + conserved[3] * conserved[3]) / density
    pressure = (HEAT_RATIO - 1.0) * (conserved[4] - kinetic)
    sound_speed = jnp.sqrt(HEAT_RATIO * pressure / density)
    momenta = [conserved[1] * velocity, conserved[2] * velocity, conserved[3] * velocity]
    momenta[direction] = momenta[direction] + pressure
    fluxes = jnp.stack([conserved[1 + direction]] + momenta + [(conserved[4] + pressure) * velocity])
    return (fluxes, jnp.abs(velocity) + sound_speed)

def face_flux(left_state, right_state, direction):
    left_flux, left_speed = one_side(left_state, direction)
    right_flux, right_speed = one_side(right_state, direction)
    wave_speed = jnp.maximum(left_speed, right_speed)
    return (0.5 * (left_flux + right_flux) - 0.5 * wave_speed[None] * (right_state - left_state), wave_speed)

def evaluate(fields, fraction, ghost_state, ghost_fraction):
    residual = jnp.zeros_like(fields)
    spectral = jnp.zeros_like(fraction)
    for direction in range(3):
        state_dim = 2 + direction
        frac_dim = 1 + direction
        padded_state = jnp.concatenate([ghost_state[2 * direction], fields, ghost_state[2 * direction + 1]], axis=state_dim)
        padded_frac = jnp.concatenate([ghost_fraction[2 * direction], fraction, ghost_fraction[2 * direction + 1]], axis=frac_dim)
        extent = padded_state.shape[state_dim]
        left_state = lax.slice_in_dim(padded_state, 0, extent - 1, axis=state_dim)
        right_state = lax.slice_in_dim(padded_state, 1, extent, axis=state_dim)
        aperture = jnp.minimum(lax.slice_in_dim(padded_frac, 0, extent - 1, axis=frac_dim), lax.slice_in_dim(padded_frac, 1, extent, axis=frac_dim))
        fluxes, wave_speed = face_flux(left_state, right_state, direction)
        weighted = aperture[None] * fluxes
        spread = aperture * wave_speed
        residual = residual + lax.slice_in_dim(weighted, 1, extent - 1, axis=state_dim) - lax.slice_in_dim(weighted, 0, extent - 2, axis=state_dim)
        spectral = spectral + lax.slice_in_dim(spread, 1, extent - 1, axis=frac_dim) + lax.slice_in_dim(spread, 0, extent - 2, axis=frac_dim)
    return (residual, spectral)

def box_sum(values, first_dim):
    for offset in range(3):
        axis_dim = first_dim + offset
        extent = values.shape[axis_dim]
        widths = [(0, 0)] * values.ndim
        widths[axis_dim] = (1, 1)
        padded = jnp.pad(values, widths)
        values = lax.slice_in_dim(padded, 0, extent, axis=axis_dim) + lax.slice_in_dim(padded, 1, extent + 1, axis=axis_dim) + lax.slice_in_dim(padded, 2, extent + 2, axis=axis_dim)
    return values

def redistribute(increment, fraction):
    volume_share = fraction[None] * increment
    return volume_share + (1.0 - fraction[None]) * box_sum(volume_share, 2) / box_sum(fraction, 1)[None]

def octants(fields):
    half_edge = BE // 2
    row_count, bricks = (fields.shape[0], fields.shape[1])
    grouped = fields.reshape(row_count, bricks, half_edge, 2, half_edge, 2, half_edge, 2)
    return grouped.sum(axis=(3, 5, 7)).reshape(row_count, bricks, half_edge ** 3)

def assemble(placed):
    half_edge = BE // 2
    row_count, bricks = (placed.shape[0], placed.shape[1])
    grouped = placed.reshape(row_count, bricks, 2, 2, 2, half_edge, half_edge, half_edge)
    return grouped.transpose(0, 1, 2, 5, 3, 6, 4, 7).reshape(row_count, bricks, BE ** 3)

def layer_of(values, face_index, first_dim):
    position = BE - 1 if face_index % 2 == 0 else 0
    return lax.slice_in_dim(values, position, position + 1, axis=first_dim + face_index // 2)

def global_ghosts(fields, fraction, neighbour):
    stream = free_stream().reshape(5, 1, 1, 1, 1)
    ghost_state = []
    ghost_fraction = []
    for face_index in range(6):
        target = neighbour[:, face_index]
        present = target >= 0
        source_index = jnp.maximum(target, 0)
        fetched = jnp.take(layer_of(fields, face_index, 2), source_index, axis=1)
        fetched_frac = jnp.take(layer_of(fraction, face_index, 1), source_index, axis=0)
        ghost_state.append(jnp.where(present.reshape(1, -1, 1, 1, 1), fetched, stream))
        ghost_fraction.append(jnp.where(present.reshape(-1, 1, 1, 1), fetched_frac, layer_of(fraction, face_index ^ 1, 1)))
    return (ghost_state, ghost_fraction)

def section_terms(fields, fraction, neighbour, final):
    ghost_state, ghost_fraction = global_ghosts(fields, fraction, neighbour)
    pieces = [(fields, 1), (fraction, 0)] + [(ghost, 1) for ghost in ghost_state] + [(ghost, 0) for ghost in ghost_fraction]
    brick_total = fraction.shape[0]

    def block_step(index, result):
        start = (index * BRICK_DEV).astype(jnp.int32)
        taken_rows = [lax.dynamic_slice_in_dim(member, start, BRICK_DEV, member_dim) for member, member_dim in pieces]
        residual, spectral = evaluate(taken_rows[0], taken_rows[1], taken_rows[2:8], taken_rows[8:14])
        if final:
            update = residual
        else:
            update = redistribute(-CFL_NUMBER * residual / spectral[None], taken_rows[1])
        return lax.dynamic_update_slice_in_dim(result, update, start, 1)
    return lax.fori_loop(0, brick_total // BRICK_DEV, block_step, jnp.zeros_like(fields))

def reference(state, volume, neighbour, parent):
    brick_total = state.shape[1]
    fields = state.reshape(5, brick_total, BE, BE, BE)
    fraction = (volume.astype(jnp.float32) / 8.0).reshape(brick_total, BE, BE, BE)
    middle = fields + FIRST_SECTION * section_terms(fields, fraction, neighbour, False)
    fine_fields = fields + section_terms(middle, fraction, neighbour, False)
    fine_residual = section_terms(fine_fields, fraction, neighbour, True)
    octant_sums = jnp.concatenate([octants(fraction[None] * fine_fields), octants(fraction[None]), octants(fine_residual)], axis=0)
    placed = jnp.zeros((11, brick_total // 8, 8, octant_sums.shape[2]), jnp.float32).at[:, parent // 8, parent % 8].set(octant_sums)
    assembled = assemble(placed)
    return (fine_fields.reshape(5, brick_total, BE ** 3), assembled[0:5] / assembled[5:6], assembled[6:11])
```

```python
import functools

import jax
import jax.numpy as jnp
from jax import lax
from jax.experimental import pallas as pl
from jax.experimental.pallas import tpu as pltpu
from jax.sharding import PartitionSpec as P

BE = 8
CUBE = 4
LANES = 128
CFL_NUMBER = 0.25
FIRST_SECTION = 0.5
STREAM = (1.0, 0.5, 0.0, 0.0, 1.0 / (1.4 * (1.4 - 1.0)) + 0.125)
f32 = jnp.float32
bf16 = jnp.bfloat16
i32 = jnp.int32
MESH = pl.DeviceIdType.MESH


def iota(shape, dim):
    return lax.broadcasted_iota(i32, shape, dim)


def pieces(x):
    hi = x.astype(bf16)
    rest = x - hi.astype(f32)
    mid = rest.astype(bf16)
    low = (rest - mid.astype(f32)).astype(bf16)
    return hi, mid, low


def dot(a, b, dims):
    return lax.dot_general(a, b, (dims, ((), ())), preferred_element_type=f32)


def prims(u):
    inv = 1.0 / u[0]
    vel = [u[1] * inv, u[2] * inv, u[3] * inv]
    kinetic = 0.5 * (u[1] * vel[0] + u[2] * vel[1] + u[3] * vel[2])
    pressure = 0.4 * (u[4] - kinetic)
    sound = jnp.sqrt(1.4 * pressure * inv)
    return vel, pressure, sound


def flux(u, v, p, k):
    out = [u[1 + k]]
    for j in range(3):
        m = u[1 + j] * v
        out.append(m + p if j == k else m)
    out.append((u[4] + p) * v)
    return out


def face(ul, vl, pl_, sl, al, ur, vr, pr, sr, ar, k, mask):
    s = jnp.maximum(sl, sr)
    a = jnp.minimum(al, ar)
    if mask is not None:
        a = jnp.where(mask, a, 0.0)
    half = 0.5 * a
    fl = flux(ul, vl, pl_, k)
    fr = flux(ur, vr, pr, k)
    w = [half * ((fl[i] + fr[i]) - s * (ur[i] - ul[i])) for i in range(5)]
    return w, a * s


def face_from(ul, al, ur, ar, k, mask=None):
    vl, pl_, cl = prims(ul)
    vr, pr, cr = prims(ur)
    return face(ul, vl[k], pl_, jnp.abs(vl[k]) + cl, al,
                ur, vr[k], pr, jnp.abs(vr[k]) + cr, ar, k, mask)


def roll(x, shift, axis):
    size = x.shape[axis]
    shift = shift % size
    return x if shift == 0 else pltpu.roll(x, shift, axis)


def kernel(n, vol_ref, nb_ref, par_ref, x_ref,
           fine_ref, cs_ref, cr_ref,
           u0, u1, res, lam, box, gain, frac_send, send, recv, csend, crecv,
           ssem, rsem, cssem, crsem):
    me = lax.axis_index("sfc")
    bits = n.bit_length() - 1
    brick = x_ref.shape[1]
    cells = BE ** 3

    coord, extent = [], []
    for k in range(3):
        value, size = 0, 1
        for i in range(bits):
            if i % 3 == k:
                value = value + (me // (1 << i)) % 2 * size
                size *= 2
        coord.append(value)
        extent.append(size)

    def device_at(axis, value):
        out = 0
        for i in range(bits):
            k = i % 3
            source = value if k == axis else coord[k]
            out = out + (source // (1 << (i // 3))) % 2 * (1 << i)
        return out

    below = [device_at(k, (coord[k] + extent[k] - 1) % extent[k]) for k in range(3)]
    above = [device_at(k, (coord[k] + 1) % extent[k]) for k in range(3)]
    nxt, prev = (me + 1) % n, (me + n - 1) % n

    barrier = pltpu.get_barrier_semaphore()
    for target in below + above + [nxt, prev]:
        pl.semaphore_signal(barrier, inc=1, device_id=(target,), device_id_type=MESH)

    nb = nb_ref[...]
    par = par_ref[...].astype(f32)
    eye = iota((brick, brick), 0) == iota((brick, brick), 1)
    par_col = jnp.sum(jnp.where(eye, par, 0.0), axis=1, keepdims=True)
    par_int = par_col.astype(i32)
    octant = par_int & 7
    remote = jnp.where((nb < 0) | (lax.div(jnp.maximum(nb, 0), brick) != me), 1, 0)

    def position(axis, parity):
        low = remote[:, 2 * axis:2 * axis + 1]
        high = remote[:, 2 * axis + 1:2 * axis + 2]
        return jnp.where(parity == 0, 2 - 2 * low, 1 + 2 * high)

    bx = position(0, octant >> 2)
    by = position(1, (octant >> 1) & 1)
    bz = position(2, octant & 1)
    lane0 = bx * 32 + by * 4 + bz
    lane2 = jnp.concatenate([lane0, lane0 + 16], axis=0)
    hot = iota((2 * brick, LANES), 1) == lane2
    perm = jnp.where(hot, 1.0, 0.0).astype(bf16)
    par_lane = jnp.sum(jnp.where(hot, jnp.concatenate([par_col, par_col], axis=0), 0.0),
                       axis=0, keepdims=True).astype(i32)

    def to_grid(x):
        both = jnp.concatenate([x[:, :cells // 2], x[:, cells // 2:]], axis=0)
        return both

    def put(f, parts):
        total = sum(dot(part, perm, ((0,), (0,))) for part in parts)
        u0[f] = total.reshape(4, 8, 8, LANES)

    put(5, [(to_grid(vol_ref[...]).astype(f32) * 0.125).astype(bf16)])
    for f in range(5):
        put(f, pieces(to_grid(x_ref[f])))

    lane = iota((1, 1, LANES), 2)
    block_x, lane_by, lane_bz = lane >> 4, (lane >> 2) & 3, lane & 3
    ixhi = (lane >> 4) & 1
    iz = iota((1, 8, LANES), 1)
    lane_l = iota((1, 8, LANES), 2)

    slot_of = (block_x, lane_by, lane_bz)
    packed_slots = (8, 4, 4)

    def source_layer(src, count, k, high, j):
        if k == 0:
            return src[0:count, 3 if high else 0, j]
        if k == 1:
            return src[0:count, j, 7 if high else 0]
        z = 7 if high else 0
        return src[0:count, j, :, z, :]

    strides = (16, 4, 1)

    def pack(src, count, k, high):
        total = None
        last = packed_slots[k] - 1
        for j in range(packed_slots[k]):
            v = source_layer(src, count, k, high, j)
            v = roll(v, strides[k] * (j - (last if high else 0)), 2)
            total = v if total is None else jnp.where(slot_of[k] == j, v, total)
        return total

    def unpack(w, k, high, j):
        last = packed_slots[k] - 1
        v = roll(w, strides[k] * ((last if high else 0) - j), w.ndim - 1)
        return v

    def exchange(stage, src):
        copies = []
        count = 6 if stage == 0 else 5
        for k in range(3):
            for high in (0, 1):
                face_index = 2 * k + high
                send[stage, face_index, 0:count] = pack(src, count, k, high)
        if stage == 0:
            pl.semaphore_wait(barrier, 8)
        for k in range(3):
            for high in (0, 1):
                mine = 2 * k + high
                copy = pltpu.make_async_remote_copy(
                    src_ref=send.at[stage, mine, pl.ds(0, count)],
                    dst_ref=recv.at[stage, 2 * k + 1 - high, pl.ds(0, count)],
                    send_sem=ssem.at[stage, mine],
                    recv_sem=rsem.at[stage, 2 * k + 1 - high],
                    device_id=((above if high else below)[k],),
                    device_id_type=MESH,
                )
                copy.start()
                copies.append(copy)
        return copies

    def shift_x(a):
        return jnp.concatenate([a[1:4], roll(a[0:1], -16, 2)], axis=0)

    def back_x(a):
        return jnp.concatenate([roll(a[3:4], 16, 2), a[0:3]], axis=0)

    def shift_y(a):
        return jnp.concatenate([a[1:8], roll(a[0:1], -4, 2)], axis=0)

    def back_y(a):
        return jnp.concatenate([roll(a[7:8], 4, 2), a[0:7]], axis=0)

    def shift_z(a):
        b = roll(a, -1, 1)
        return jnp.where(iz == 7, roll(b, -1, 2), b)

    def back_z(a):
        b = roll(a, 1, 1)
        return jnp.where(iz == 0, roll(b, 1, 2), b)

    slab = iota((4, 1, LANES), 0)
    mask_x = jnp.logical_not((slab == 3) & (block_x == 7))
    row = iota((8, 1, LANES), 0)
    mask_y = jnp.logical_not((row == 7) & (lane_by == 3))
    mask_z = jnp.logical_not((iz == 7) & ((lane_l & 3) == 3))

    def interior(src, want_lam):
        def pass_xz(y, carry):
            u = [src[f, :, y] for f in range(5)]
            a = u0[5, :, y]
            vel, p, c = prims(u)
            total = spread = None
            for k, ahead, back, mask in ((0, shift_x, back_x, mask_x), (2, shift_z, back_z, mask_z)):
                speed = jnp.abs(vel[k]) + c
                w, s = face(u, vel[k], p, speed, a,
                            [ahead(q) for q in u], ahead(vel[k]), ahead(p), ahead(speed), ahead(a),
                            k, mask)
                diff = [q - back(q) for q in w]
                total = diff if total is None else [t + d for t, d in zip(total, diff)]
                if want_lam:
                    both = s + back(s)
                    spread = both if spread is None else spread + both
            for f in range(5):
                res[f, :, y] = total[f]
            if want_lam:
                lam[:, y] = spread
            return carry

        lax.fori_loop(0, 8, pass_xz, 0)

        def pass_y(x, carry):
            u = [src[f, x] for f in range(5)]
            a = u0[5, x]
            vel, p, c = prims(u)
            speed = jnp.abs(vel[1]) + c
            w, s = face(u, vel[1], p, speed, a,
                        [shift_y(q) for q in u], shift_y(vel[1]), shift_y(p), shift_y(speed), shift_y(a),
                        1, mask_y)
            for f in range(5):
                res[f, x] = res[f, x] + (w[f] - back_y(w[f]))
            if want_lam:
                lam[x] = lam[x] + (s + back_y(s))
            return carry

        lax.fori_loop(0, 4, pass_y, 0)

    def boundary(stage, copies, want_lam):
        for copy in copies:
            copy.wait()
        for k in range(3):
            for high in (0, 1):
                index = 2 * k + high
                own_u = [send[stage, index, f] for f in range(5)]
                own_a = send[0, index, 5]
                other_u = [recv[stage, index, f] for f in range(5)]
                other_a = recv[0, index, 5]
                if k != 1:
                    at_end = coord[k] == (extent[k] - 1 if high else 0)
                    other_u = [jnp.where(at_end, STREAM[f], other_u[f]) for f in range(5)]
                    other_a = jnp.where(at_end, own_a, other_a)
                if high:
                    w, s = face_from(own_u, own_a, other_u, other_a, k)
                    sign = 1.0
                else:
                    w, s = face_from(other_u, other_a, own_u, own_a, k)
                    sign = -1.0
                edge = packed_slots[k] - 1 if high else 0
                values = jnp.stack([sign * q for q in w] + ([s] if want_lam else []), axis=0)
                here = slot_of[k] == edge
                for j in range(packed_slots[k]):
                    add = jnp.where(here, unpack(values, k, high, j), 0.0)
                    if k == 0:
                        at = (3 if high else 0, j)
                    elif k == 1:
                        at = (j, 7 if high else 0)
                    else:
                        at = (j, slice(None), 7 if high else 0, slice(None))
                    where5 = (slice(0, 5),) + at
                    res[where5] = res[where5] + add[0:5]
                    if want_lam:
                        lam[at] = lam[at] + add[5]

    def box_x(a):
        up = jnp.where(ixhi == 0, roll(a[0:1], -16, 2), 0.0)
        down = jnp.where(ixhi == 1, roll(a[3:4], 16, 2), 0.0)
        return a + jnp.concatenate([a[1:4], up], axis=0) + jnp.concatenate([down, a[0:3]], axis=0)

    def box_y(a):
        zero = jnp.zeros_like(a[0:1])
        return a + jnp.concatenate([a[1:8], zero], axis=0) + jnp.concatenate([zero, a[0:7]], axis=0)

    def box_z(a):
        return a + jnp.where(iz == 7, 0.0, roll(a, -1, 1)) + jnp.where(iz == 0, 0.0, roll(a, 1, 1))

    def box_of_frac():
        def first(y, carry):
            box[0, :, y] = box_z(box_x(u0[5, :, y]))
            return carry
        lax.fori_loop(0, 8, first, 0)

        def second(x, carry):
            gain[x] = (1.0 - u0[5, x]) / box_y(box[0, x])
            return carry
        lax.fori_loop(0, 4, second, 0)

    def update(factor):
        def first(y, carry):
            share = u0[5, :, y] * (-CFL_NUMBER / lam[:, y])
            for f in range(5):
                d = share * res[f, :, y]
                res[f, :, y] = d
                box[f, :, y] = box_z(box_x(d))
            return carry
        lax.fori_loop(0, 8, first, 0)

        def second(x, carry):
            g = gain[x]
            for f in range(5):
                u1[f, x] = u0[f, x] + factor * (res[f, x] + g * box_y(box[f, x]))
            return carry
        lax.fori_loop(0, 4, second, 0)

    copies0 = exchange(0, u0)
    box_of_frac()
    interior(u0, True)
    boundary(0, copies0, True)
    update(FIRST_SECTION)

    copies1 = exchange(1, u1)
    interior(u1, True)
    boundary(1, copies1, True)
    update(1.0)

    copies2 = exchange(2, u1)

    c = iota((LANES, 256), 0)
    col = iota((LANES, 256), 1)
    rowc = col & 63
    spread = (((c >> 6) == (rowc >> 5)) & (((c >> 3) & 3) == ((rowc >> 3) & 3))
              & ((rowc & 7) == 2 * (c & 3))
              & (((c >> 5) & 1) == (col >> 7)) & (((c >> 2) & 1) == ((col >> 6) & 1)))
    spread = jnp.where(spread, 1.0, 0.0).astype(bf16)
    r = iota((64, LANES), 0)
    ln = iota((64, LANES), 1)
    coarse_base = jnp.where(r >= 32, nxt, me) * (brick // 8)
    pick = ((((r >> 3) & 3) == ((ln >> 4) & 3))
            & (jnp.broadcast_to(par_lane >> 3, (64, LANES)) == coarse_base + (r & 7)))
    pick = jnp.where(pick, 1.0, 0.0).astype(bf16)
    lane2d = iota((1, LANES), 1)
    which = ((lane2d >> 2) & 1) * 2 + (lane2d & 1)

    def sums(x):
        g = x.reshape(2, 2, 4, 2, 8, LANES)
        s = (g[:, 0, :, 0] + g[:, 0, :, 1]) + (g[:, 1, :, 0] + g[:, 1, :, 1])
        s = s.reshape(8, 8, LANES)
        return s + roll(s, -1, 1)

    def place(s):
        flat = s.reshape(64, LANES)
        stacked = jnp.concatenate([jnp.where(which == o, flat, 0.0) for o in range(4)], axis=0)
        z = sum(dot(spread, part, ((1,), (0,))) for part in pieces(stacked))
        return sum(dot(pick, part, ((1,), (1,))) for part in pieces(z))

    def coarse(group, f, s, out):
        placed = place(s)
        csend[group, f] = placed[32:64]
        for t in range(4):
            out[f, :, t * LANES:(t + 1) * LANES] = placed[8 * t:8 * t + 8]

    def coarse_copy(group):
        copy = pltpu.make_async_remote_copy(
            src_ref=csend.at[group], dst_ref=crecv.at[group],
            send_sem=cssem.at[group], recv_sem=crsem.at[group],
            device_id=(nxt,), device_id_type=MESH)
        copy.start()
        return copy

    def coarse_finish(group, copy, out):
        copy.wait()
        for f in range(5):
            for t in range(4):
                at = (f, slice(None), slice(t * LANES, (t + 1) * LANES))
                out[at] = out[at] + crecv[group, f, 8 * t:8 * t + 8]

    inv = 1.0 / sums(u0[5])
    for f in range(5):
        coarse(0, f, sums(u0[5] * u1[f]) * inv, cs_ref)
    state_copy = coarse_copy(0)

    interior(u1, False)

    boundary(2, copies2, False)
    for f in range(5):
        coarse(1, f, sums(res[f]), cr_ref)
    residual_copy = coarse_copy(1)

    for f in range(5):
        flat = u1[f].reshape(256, LANES)
        back = sum(dot(perm, part, ((1,), (1,))) for part in pieces(flat))
        fine_ref[f, :, 0:256] = back[0:brick]
        fine_ref[f, :, 256:512] = back[brick:2 * brick]

    coarse_finish(0, state_copy, cs_ref)
    coarse_finish(1, residual_copy, cr_ref)


def local(n, state, volume, neighbour, parent):
    brick = state.shape[1]
    grid = (4, 8, 8, LANES)
    vmem = pl.BlockSpec(memory_space=pltpu.VMEM)
    coarse_shape = jax.ShapeDtypeStruct((5, brick // 8, BE ** 3), f32)
    return pl.pallas_call(
        functools.partial(kernel, n),
        out_shape=(jax.ShapeDtypeStruct(state.shape, f32), coarse_shape, coarse_shape),
        in_specs=[vmem] * 4,
        out_specs=(vmem,) * 3,
        scratch_shapes=[
            pltpu.VMEM((6,) + grid, f32),
            pltpu.VMEM((5,) + grid, f32),
            pltpu.VMEM((5,) + grid, f32),
            pltpu.VMEM(grid, f32),
            pltpu.VMEM((5,) + grid, f32),
            pltpu.VMEM(grid, f32),
            pltpu.VMEM((8, LANES), f32),
            pltpu.VMEM((3, 6, 6, 8, LANES), f32),
            pltpu.VMEM((3, 6, 6, 8, LANES), f32),
            pltpu.VMEM((2, 5, 32, LANES), f32),
            pltpu.VMEM((2, 5, 32, LANES), f32),
            pltpu.SemaphoreType.DMA((3, 6)),
            pltpu.SemaphoreType.DMA((3, 6)),
            pltpu.SemaphoreType.DMA((2,)),
            pltpu.SemaphoreType.DMA((2,)),
        ],
        compiler_params=pltpu.CompilerParams(
            collective_id=0, has_side_effects=True, vmem_limit_bytes=40 * 1024 * 1024),
    )(volume, neighbour, parent.reshape(1, brick), state)


def solution(mesh):
    in_specs = (P(None, "sfc", None), P("sfc", None), P("sfc", None), P("sfc"))
    out_specs = (P(None, "sfc", None), P(None, "sfc", None), P(None, "sfc", None))
    return jax.shard_map(functools.partial(local, mesh.shape["sfc"]), mesh=mesh,
                         in_specs=in_specs, out_specs=out_specs, check_vma=False)
```

```python
import functools

import jax
import jax.numpy as jnp
from jax import lax
from jax.experimental import pallas as pl
from jax.experimental.pallas import tpu as pltpu
from jax.sharding import PartitionSpec as P

BE = 8
CUBE = 4
LANES = 128
CFL_NUMBER = 0.25
FIRST_SECTION = 0.5
STREAM = (1.0, 0.5, 0.0, 0.0, 1.0 / (1.4 * (1.4 - 1.0)) + 0.125)
f32 = jnp.float32
bf16 = jnp.bfloat16
i32 = jnp.int32
MESH = pl.DeviceIdType.MESH


def iota(shape, dim):
    return lax.broadcasted_iota(i32, shape, dim)


def pieces(x):
    hi = x.astype(bf16)
    rest = x - hi.astype(f32)
    mid = rest.astype(bf16)
    low = (rest - mid.astype(f32)).astype(bf16)
    return hi, mid, low


def dot(a, b, dims):
    return lax.dot_general(a, b, (dims, ((), ())), preferred_element_type=f32)


def prims(u):
    inv = 1.0 / u[0]
    vel = [u[1] * inv, u[2] * inv, u[3] * inv]
    kinetic = 0.5 * (u[1] * vel[0] + u[2] * vel[1] + u[3] * vel[2])
    pressure = 0.4 * (u[4] - kinetic)
    sound = jnp.sqrt(1.4 * pressure * inv)
    return vel, pressure, sound


def flux(u, v, p, k):
    out = [u[1 + k]]
    for j in range(3):
        m = u[1 + j] * v
        out.append(m + p if j == k else m)
    out.append((u[4] + p) * v)
    return out


def face(ul, vl, pl_, sl, al, ur, vr, pr, sr, ar, k, mask):
    s = jnp.maximum(sl, sr)
    a = jnp.minimum(al, ar)
    if mask is not None:
        a = jnp.where(mask, a, 0.0)
    half = 0.5 * a
    fl = flux(ul, vl, pl_, k)
    fr = flux(ur, vr, pr, k)
    w = [half * ((fl[i] + fr[i]) - s * (ur[i] - ul[i])) for i in range(5)]
    return w, a * s


def face_from(ul, al, ur, ar, k, mask=None):
    vl, pl_, cl = prims(ul)
    vr, pr, cr = prims(ur)
    return face(ul, vl[k], pl_, jnp.abs(vl[k]) + cl, al,
                ur, vr[k], pr, jnp.abs(vr[k]) + cr, ar, k, mask)


def roll(x, shift, axis):
    size = x.shape[axis]
    shift = shift % size
    return x if shift == 0 else pltpu.roll(x, shift, axis)


def kernel(n, vol_hbm, nb_ref, par_ref, x_hbm,
           fine_ref, cs_ref, cr_ref,
           vol_ref, x_ref, in_sem, u0, u1, res, lam, box, gain, send, recv, csend, crecv,
           ssem, rsem, cssem, crsem):
    me = lax.axis_index("sfc")
    bits = n.bit_length() - 1
    brick = x_ref.shape[1]
    cells = BE ** 3

    loads = [pltpu.make_async_copy(vol_hbm, vol_ref, in_sem.at[5])]
    for f in range(5):
        loads.append(pltpu.make_async_copy(x_hbm.at[f], x_ref.at[f], in_sem.at[f]))
    for load in loads:
        load.start()

    coord, extent = [], []
    for k in range(3):
        value, size = 0, 1
        for i in range(bits):
            if i % 3 == k:
                value = value + (me // (1 << i)) % 2 * size
                size *= 2
        coord.append(value)
        extent.append(size)

    def device_at(axis, value):
        out = 0
        for i in range(bits):
            k = i % 3
            source = value if k == axis else coord[k]
            out = out + (source // (1 << (i // 3))) % 2 * (1 << i)
        return out

    below = [device_at(k, (coord[k] + extent[k] - 1) % extent[k]) for k in range(3)]
    above = [device_at(k, (coord[k] + 1) % extent[k]) for k in range(3)]
    nxt, prev = (me + 1) % n, (me + n - 1) % n

    barrier = pltpu.get_barrier_semaphore()
    for target in below + above + [nxt, prev]:
        pl.semaphore_signal(barrier, inc=1, device_id=(target,), device_id_type=MESH)

    nb = nb_ref[...]
    par = par_ref[...]
    octant = par & 7
    remote = jnp.where((nb < 0) | (lax.div(jnp.maximum(nb, 0), brick) != me), 1, 0)

    def position(axis, parity):
        low = remote[2 * axis:2 * axis + 1]
        high = remote[2 * axis + 1:2 * axis + 2]
        return jnp.where(parity == 0, 2 - 2 * low, 1 + 2 * high)

    bx = position(0, octant >> 2)
    by = position(1, (octant >> 1) & 1)
    bz = position(2, octant & 1)
    eye = iota((brick, brick), 0) == iota((brick, brick), 1)

    def column(r):
        return jnp.sum(jnp.where(eye, r.astype(f32), 0.0), axis=1, keepdims=True)

    par_col = column(par)
    lane0 = column(bx * 32 + by * 4 + bz).astype(i32)
    lane2 = jnp.concatenate([lane0, lane0 + 16], axis=0)
    hot = iota((2 * brick, LANES), 1) == lane2
    perm = jnp.where(hot, 1.0, 0.0).astype(bf16)
    par_lane = jnp.sum(jnp.where(hot, jnp.concatenate([par_col, par_col], axis=0), 0.0),
                       axis=0, keepdims=True).astype(i32)

    def to_grid(x):
        both = jnp.concatenate([x[:, :cells // 2], x[:, cells // 2:]], axis=0)
        return both

    perm2 = jnp.concatenate([perm, perm], axis=0)
    loads[0].wait()
    volume = (to_grid(vol_ref[...]).astype(f32) * 0.125).astype(bf16)
    u0[5] = dot(volume, perm, ((0,), (0,))).reshape(4, 8, 8, LANES)
    for f in range(5):
        loads[1 + f].wait()
        hi, mid, low = pieces(to_grid(x_ref[f]))
        total = (dot(jnp.concatenate([hi, mid], axis=0), perm2, ((0,), (0,)))
                 + dot(low, perm, ((0,), (0,))))
        u0[f] = total.reshape(4, 8, 8, LANES)

    lane = iota((1, 1, LANES), 2)
    block_x, lane_by, lane_bz = lane >> 4, (lane >> 2) & 3, lane & 3
    ixhi = (lane >> 4) & 1
    iz = iota((1, 8, LANES), 1)
    lane_l = iota((1, 8, LANES), 2)

    slot_of = (block_x, lane_by, lane_bz)
    packed_slots = (8, 4, 4)

    def source_layer(src, count, k, high, j):
        if k == 0:
            return src[0:count, 3 if high else 0, j]
        if k == 1:
            return src[0:count, j, 7 if high else 0]
        z = 7 if high else 0
        return src[0:count, j, :, z, :]

    strides = (16, 4, 1)

    def pack(src, count, k, high):
        total = None
        last = packed_slots[k] - 1
        for j in range(packed_slots[k]):
            v = source_layer(src, count, k, high, j)
            v = roll(v, strides[k] * (j - (last if high else 0)), 2)
            total = v if total is None else jnp.where(slot_of[k] == j, v, total)
        return total

    def unpack(w, k, high, j):
        last = packed_slots[k] - 1
        v = roll(w, strides[k] * ((last if high else 0) - j), w.ndim - 1)
        return v

    def exchange(stage, src):
        copies = []
        count = 6 if stage == 0 else 5
        for k in range(3):
            for high in (0, 1):
                face_index = 2 * k + high
                send[stage, face_index, 0:count] = pack(src, count, k, high)
        if stage == 0:
            pl.semaphore_wait(barrier, 8)
        for k in range(3):
            for high in (0, 1):
                mine = 2 * k + high
                copy = pltpu.make_async_remote_copy(
                    src_ref=send.at[stage, mine, pl.ds(0, count)],
                    dst_ref=recv.at[stage, 2 * k + 1 - high, pl.ds(0, count)],
                    send_sem=ssem.at[stage, mine],
                    recv_sem=rsem.at[stage, 2 * k + 1 - high],
                    device_id=((above if high else below)[k],),
                    device_id_type=MESH,
                )
                copy.start()
                copies.append(copy)
        return copies

    def shift_x(a):
        return jnp.concatenate([a[1:4], roll(a[0:1], -16, 2)], axis=0)

    def back_x(a):
        return jnp.concatenate([roll(a[3:4], 16, 2), a[0:3]], axis=0)

    def shift_y(a):
        return jnp.concatenate([a[1:8], roll(a[0:1], -4, 2)], axis=0)

    def back_y(a):
        return jnp.concatenate([roll(a[7:8], 4, 2), a[0:7]], axis=0)

    def shift_z(a):
        b = roll(a, -1, 1)
        return jnp.where(iz == 7, roll(b, -1, 2), b)

    def back_z(a):
        b = roll(a, 1, 1)
        return jnp.where(iz == 0, roll(b, 1, 2), b)

    slab = iota((4, 1, LANES), 0)
    mask_x = jnp.logical_not((slab == 3) & (block_x == 7))
    row = iota((8, 1, LANES), 0)
    mask_y = jnp.logical_not((row == 7) & (lane_by == 3))
    mask_z = jnp.logical_not((iz == 7) & ((lane_l & 3) == 3))

    def interior(src, want_lam):
        def pass_xz(y, carry):
            u = [src[f, :, y] for f in range(5)]
            a = u0[5, :, y]
            vel, p, c = prims(u)
            total = spread = None
            for k, ahead, back, mask in ((0, shift_x, back_x, mask_x), (2, shift_z, back_z, mask_z)):
                speed = jnp.abs(vel[k]) + c
                w, s = face(u, vel[k], p, speed, a,
                            [ahead(q) for q in u], ahead(vel[k]), ahead(p), ahead(speed), ahead(a),
                            k, mask)
                diff = [q - back(q) for q in w]
                total = diff if total is None else [t + d for t, d in zip(total, diff)]
                if want_lam:
                    both = s + back(s)
                    spread = both if spread is None else spread + both
            for f in range(5):
                res[f, :, y] = total[f]
            if want_lam:
                lam[:, y] = spread
            return carry

        lax.fori_loop(0, 8, pass_xz, 0)

        def pass_y(x, carry):
            u = [src[f, x] for f in range(5)]
            a = u0[5, x]
            vel, p, c = prims(u)
            speed = jnp.abs(vel[1]) + c
            w, s = face(u, vel[1], p, speed, a,
                        [shift_y(q) for q in u], shift_y(vel[1]), shift_y(p), shift_y(speed), shift_y(a),
                        1, mask_y)
            for f in range(5):
                res[f, x] = res[f, x] + (w[f] - back_y(w[f]))
            if want_lam:
                lam[x] = lam[x] + (s + back_y(s))
            return carry

        lax.fori_loop(0, 4, pass_y, 0)

    def boundary(stage, copies, want_lam):
        for copy in copies:
            copy.wait()
        for k in range(3):
            for high in (0, 1):
                index = 2 * k + high
                own_u = [send[stage, index, f] for f in range(5)]
                own_a = send[0, index, 5]
                other_u = [recv[stage, index, f] for f in range(5)]
                other_a = recv[0, index, 5]
                if k != 1:
                    at_end = coord[k] == (extent[k] - 1 if high else 0)
                    other_u = [jnp.where(at_end, STREAM[f], other_u[f]) for f in range(5)]
                    other_a = jnp.where(at_end, own_a, other_a)
                if high:
                    w, s = face_from(own_u, own_a, other_u, other_a, k)
                    sign = 1.0
                else:
                    w, s = face_from(other_u, other_a, own_u, own_a, k)
                    sign = -1.0
                edge = packed_slots[k] - 1 if high else 0
                values = jnp.stack([sign * q for q in w] + ([s] if want_lam else []), axis=0)
                here = slot_of[k] == edge
                for j in range(packed_slots[k]):
                    add = jnp.where(here, unpack(values, k, high, j), 0.0)
                    if k == 0:
                        at = (3 if high else 0, j)
                    elif k == 1:
                        at = (j, 7 if high else 0)
                    else:
                        at = (j, slice(None), 7 if high else 0, slice(None))
                    where5 = (slice(0, 5),) + at
                    res[where5] = res[where5] + add[0:5]
                    if want_lam:
                        lam[at] = lam[at] + add[5]

    def box_x(a):
        up = jnp.where(ixhi == 0, roll(a[0:1], -16, 2), 0.0)
        down = jnp.where(ixhi == 1, roll(a[3:4], 16, 2), 0.0)
        return a + jnp.concatenate([a[1:4], up], axis=0) + jnp.concatenate([down, a[0:3]], axis=0)

    def box_y(a):
        zero = jnp.zeros_like(a[0:1])
        return a + jnp.concatenate([a[1:8], zero], axis=0) + jnp.concatenate([zero, a[0:7]], axis=0)

    def box_z(a):
        return a + jnp.where(iz == 7, 0.0, roll(a, -1, 1)) + jnp.where(iz == 0, 0.0, roll(a, 1, 1))

    def box_of_frac():
        def first(y, carry):
            box[0, :, y] = box_z(box_x(u0[5, :, y]))
            return carry
        lax.fori_loop(0, 8, first, 0)

        def second(x, carry):
            gain[x] = (1.0 - u0[5, x]) / box_y(box[0, x])
            return carry
        lax.fori_loop(0, 4, second, 0)

    def update(factor):
        def first(y, carry):
            share = u0[5, :, y] * (-CFL_NUMBER / lam[:, y])
            for f in range(5):
                d = share * res[f, :, y]
                res[f, :, y] = d
                box[f, :, y] = box_z(box_x(d))
            return carry
        lax.fori_loop(0, 8, first, 0)

        def second(x, carry):
            g = gain[x]
            for f in range(5):
                u1[f, x] = u0[f, x] + factor * (res[f, x] + g * box_y(box[f, x]))
            return carry
        lax.fori_loop(0, 4, second, 0)

    copies0 = exchange(0, u0)
    box_of_frac()
    interior(u0, True)
    boundary(0, copies0, True)
    update(FIRST_SECTION)

    copies1 = exchange(1, u1)
    interior(u1, True)
    boundary(1, copies1, True)
    update(1.0)

    copies2 = exchange(2, u1)

    r = iota((64, LANES), 0)
    ln = iota((64, LANES), 1)
    coarse_base = jnp.where(r >= 32, nxt, me) * (brick // 8)
    pick = ((((r >> 3) & 3) == ((ln >> 4) & 3))
            & (jnp.broadcast_to(par_lane >> 3, (64, LANES)) == coarse_base + (r & 7)))
    pick = jnp.where(pick, 1.0, 0.0).astype(bf16)
    pick2 = jnp.concatenate([pick, pick], axis=1)
    lane_oy, lane_oz = (lane >> 2) & 1, lane & 1
    sub = iota((1, 8, LANES), 1)
    same_oz = (sub >> 2) == lane_oz

    def sums(x):
        g = x.reshape(2, 2, 4, 2, 8, LANES)
        s = (g[:, 0, :, 0] + g[:, 0, :, 1]) + (g[:, 1, :, 0] + g[:, 1, :, 1])
        s = s.reshape(8, 8, LANES)
        return s + roll(s, -1, 1)

    def coarse_rows(s):
        t = s
        for j in range(1, 4):
            t = jnp.where(sub == j, roll(s, -j, 1), t)
        t = jnp.where(sub >= 4, roll(t, 4, 1), t)
        t = jnp.where(same_oz, t, 0.0)
        both = [jnp.where(lane_oy == oy, t, 0.0) for oy in range(2)]
        return jnp.concatenate([both[0][0:4], both[1][0:4], both[0][4:8], both[1][4:8]],
                               axis=0).reshape(LANES, LANES)

    def coarse(group, values, out):
        z = jnp.concatenate([coarse_rows(s) for s in values], axis=0)
        hi, mid, _ = pieces(z)
        placed = dot(pick2, jnp.concatenate([hi, mid], axis=1), ((1,), (1,)))
        for f in range(5):
            block = placed[:, f * LANES:(f + 1) * LANES]
            csend[group, f] = block[32:64]
            for t in range(4):
                out[f, :, t * LANES:(t + 1) * LANES] = block[8 * t:8 * t + 8]

    def coarse_copy(group):
        copy = pltpu.make_async_remote_copy(
            src_ref=csend.at[group], dst_ref=crecv.at[group],
            send_sem=cssem.at[group], recv_sem=crsem.at[group],
            device_id=(nxt,), device_id_type=MESH)
        copy.start()
        return copy

    def coarse_finish(group, copy, out):
        copy.wait()
        for f in range(5):
            for t in range(4):
                at = (f, slice(None), slice(t * LANES, (t + 1) * LANES))
                out[at] = out[at] + crecv[group, f, 8 * t:8 * t + 8]

    inv = 1.0 / sums(u0[5])
    coarse(0, [sums(u0[5] * u1[f]) * inv for f in range(5)], cs_ref)
    state_copy = coarse_copy(0)

    interior(u1, False)

    boundary(2, copies2, False)
    coarse(1, [sums(res[f]) for f in range(5)], cr_ref)
    residual_copy = coarse_copy(1)

    perm_wide = jnp.concatenate([perm, perm], axis=1)
    for f in range(5):
        hi, mid, _ = pieces(u1[f].reshape(256, LANES))
        back = dot(perm_wide, jnp.concatenate([hi, mid], axis=1), ((1,), (1,)))
        fine_ref[f, :, 0:256] = back[0:brick]
        fine_ref[f, :, 256:512] = back[brick:2 * brick]

    coarse_finish(0, state_copy, cs_ref)
    coarse_finish(1, residual_copy, cr_ref)


def write_out(*refs):
    sources, targets, sem = refs[:3], refs[3:6], refs[6]
    copies = [pltpu.make_async_copy(sources[i], targets[i], sem.at[i]) for i in range(3)]
    for copy in copies:
        copy.start()
    for copy in copies:
        copy.wait()


def local(n, state, volume, neighbour, parent):
    brick = state.shape[1]
    grid = (4, 8, 8, LANES)
    vmem = pl.BlockSpec(memory_space=pltpu.VMEM)
    hbm = pl.BlockSpec(memory_space=pltpu.HBM)
    coarse_shape = jax.ShapeDtypeStruct((5, brick // 8, BE ** 3), f32)
    shapes = (jax.ShapeDtypeStruct(state.shape, f32), coarse_shape, coarse_shape)
    held = pl.pallas_call(
        functools.partial(kernel, n),
        out_shape=tuple(pltpu.VMEM(one.shape, one.dtype) for one in shapes),
        in_specs=[hbm, vmem, vmem, hbm],
        out_specs=(vmem,) * 3,
        scratch_shapes=[
            pltpu.VMEM(volume.shape, i32),
            pltpu.VMEM(state.shape, f32),
            pltpu.SemaphoreType.DMA((6,)),
            pltpu.VMEM((6,) + grid, f32),
            pltpu.VMEM((5,) + grid, f32),
            pltpu.VMEM((5,) + grid, f32),
            pltpu.VMEM(grid, f32),
            pltpu.VMEM((5,) + grid, f32),
            pltpu.VMEM(grid, f32),
            pltpu.VMEM((3, 6, 6, 8, LANES), f32),
            pltpu.VMEM((3, 6, 6, 8, LANES), f32),
            pltpu.VMEM((2, 5, 32, LANES), f32),
            pltpu.VMEM((2, 5, 32, LANES), f32),
            pltpu.SemaphoreType.DMA((3, 6)),
            pltpu.SemaphoreType.DMA((3, 6)),
            pltpu.SemaphoreType.DMA((2,)),
            pltpu.SemaphoreType.DMA((2,)),
        ],
        compiler_params=pltpu.CompilerParams(
            collective_id=0, has_side_effects=True, vmem_limit_bytes=60 * 1024 * 1024),
    )(volume, neighbour.T, parent.reshape(1, brick), state)
    return pl.pallas_call(
        write_out,
        out_shape=shapes,
        in_specs=[vmem] * 3,
        out_specs=(hbm,) * 3,
        scratch_shapes=[pltpu.SemaphoreType.DMA((3,))],
        compiler_params=pltpu.CompilerParams(vmem_limit_bytes=4 * 1024 * 1024),
    )(*held)


def solution(mesh):
    in_specs = (P(None, "sfc", None), P("sfc", None), P("sfc", None), P("sfc"))
    out_specs = (P(None, "sfc", None), P(None, "sfc", None), P(None, "sfc", None))
    return jax.shard_map(functools.partial(local, mesh.shape["sfc"]), mesh=mesh,
                         in_specs=in_specs, out_specs=out_specs, check_vma=False)
```

```python
import functools

import jax
import jax.numpy as jnp
from jax import lax
from jax.experimental import pallas as pl
from jax.experimental.pallas import tpu as pltpu
from jax.sharding import PartitionSpec as P

BE = 8
CUBE = 4
LANES = 128
CFL_NUMBER = 0.25
FIRST_SECTION = 0.5
STREAM = (1.0, 0.5, 0.0, 0.0, 1.0 / (1.4 * (1.4 - 1.0)) + 0.125)
f32 = jnp.float32
bf16 = jnp.bfloat16
i32 = jnp.int32
MESH = pl.DeviceIdType.MESH


def iota(shape, dim):
    return lax.broadcasted_iota(i32, shape, dim)


def pieces(x):
    hi = x.astype(bf16)
    rest = x - hi.astype(f32)
    mid = rest.astype(bf16)
    low = (rest - mid.astype(f32)).astype(bf16)
    return hi, mid, low


def dot(a, b, dims):
    return lax.dot_general(a, b, (dims, ((), ())), preferred_element_type=f32)


def prims(u):
    inv = 1.0 / u[0]
    vel = [u[1] * inv, u[2] * inv, u[3] * inv]
    kinetic = 0.5 * (u[1] * vel[0] + u[2] * vel[1] + u[3] * vel[2])
    pressure = 0.4 * (u[4] - kinetic)
    sound = jnp.sqrt(1.4 * pressure * inv)
    return vel, pressure, sound


def flux(u, v, p, k):
    out = [u[1 + k]]
    for j in range(3):
        m = u[1 + j] * v
        out.append(m + p if j == k else m)
    out.append((u[4] + p) * v)
    return out


def face(ul, vl, pl_, sl, al, ur, vr, pr, sr, ar, k, mask):
    s = jnp.maximum(sl, sr)
    a = jnp.minimum(al, ar)
    if mask is not None:
        a = jnp.where(mask, a, 0.0)
    half = 0.5 * a
    fl = flux(ul, vl, pl_, k)
    fr = flux(ur, vr, pr, k)
    w = [half * ((fl[i] + fr[i]) - s * (ur[i] - ul[i])) for i in range(5)]
    return w, a * s


def face_from(ul, al, ur, ar, k, mask=None):
    vl, pl_, cl = prims(ul)
    vr, pr, cr = prims(ur)
    return face(ul, vl[k], pl_, jnp.abs(vl[k]) + cl, al,
                ur, vr[k], pr, jnp.abs(vr[k]) + cr, ar, k, mask)


def roll(x, shift, axis):
    size = x.shape[axis]
    shift = shift % size
    return x if shift == 0 else pltpu.roll(x, shift, axis)


def kernel(n, vol_hbm, nb_ref, par_ref, x_hbm,
           fine_ref, cs_ref, cr_ref,
           vol_ref, x_ref, in_sem, u0, u1, res, lam, box, gain, send, recv, csend, crecv,
           ssem, rsem, cssem, crsem):
    me = lax.axis_index("sfc")
    bits = n.bit_length() - 1
    brick = x_ref.shape[1]
    cells = BE ** 3

    loads = [pltpu.make_async_copy(vol_hbm, vol_ref, in_sem.at[5])]
    for f in range(5):
        loads.append(pltpu.make_async_copy(x_hbm.at[f], x_ref.at[f], in_sem.at[f]))
    for load in loads:
        load.start()

    coord, extent = [], []
    for k in range(3):
        value, size = 0, 1
        for i in range(bits):
            if i % 3 == k:
                value = value + (me // (1 << i)) % 2 * size
                size *= 2
        coord.append(value)
        extent.append(size)

    def device_at(axis, value):
        out = 0
        for i in range(bits):
            k = i % 3
            source = value if k == axis else coord[k]
            out = out + (source // (1 << (i // 3))) % 2 * (1 << i)
        return out

    below = [device_at(k, (coord[k] + extent[k] - 1) % extent[k]) for k in range(3)]
    above = [device_at(k, (coord[k] + 1) % extent[k]) for k in range(3)]
    nxt, prev = (me + 1) % n, (me + n - 1) % n

    barrier = pltpu.get_barrier_semaphore()
    for target in below + above + [nxt, prev]:
        pl.semaphore_signal(barrier, inc=1, device_id=(target,), device_id_type=MESH)

    nb = nb_ref[...]
    par = par_ref[...]
    octant = par & 7
    remote = jnp.where((nb < 0) | (lax.div(jnp.maximum(nb, 0), brick) != me), 1, 0)

    def position(axis, parity):
        low = remote[2 * axis:2 * axis + 1]
        high = remote[2 * axis + 1:2 * axis + 2]
        return jnp.where(parity == 0, 2 - 2 * low, 1 + 2 * high)

    bx = position(0, octant >> 2)
    by = position(1, (octant >> 1) & 1)
    bz = position(2, octant & 1)
    eye = iota((brick, brick), 0) == iota((brick, brick), 1)

    def column(r):
        return jnp.sum(jnp.where(eye, r.astype(f32), 0.0), axis=1, keepdims=True)

    par_col = column(par)
    lane0 = column(bx * 32 + by * 4 + bz).astype(i32)
    lane2 = jnp.concatenate([lane0, lane0 + 16], axis=0)
    hot = iota((2 * brick, LANES), 1) == lane2
    perm = jnp.where(hot, 1.0, 0.0).astype(bf16)
    par_lane = jnp.sum(jnp.where(hot, jnp.concatenate([par_col, par_col], axis=0), 0.0),
                       axis=0, keepdims=True).astype(i32)

    def to_grid(x):
        both = jnp.concatenate([x[:, :cells // 2], x[:, cells // 2:]], axis=0)
        return both

    perm2 = jnp.concatenate([perm, perm], axis=0)
    loads[0].wait()
    volume = (to_grid(vol_ref[...]).astype(f32) * 0.125).astype(bf16)
    u0[5] = dot(volume, perm, ((0,), (0,))).reshape(4, 8, 8, LANES)
    for f in range(5):
        loads[1 + f].wait()
        hi, mid, low = pieces(to_grid(x_ref[f]))
        total = (dot(jnp.concatenate([hi, mid], axis=0), perm2, ((0,), (0,)))
                 + dot(low, perm, ((0,), (0,))))
        u0[f] = total.reshape(4, 8, 8, LANES)

    lane = iota((1, 1, LANES), 2)
    block_x, lane_by, lane_bz = lane >> 4, (lane >> 2) & 3, lane & 3
    ixhi = (lane >> 4) & 1
    iz = iota((1, 8, LANES), 1)
    lane_l = iota((1, 8, LANES), 2)

    slot_of = (block_x, lane_by, lane_bz)
    packed_slots = (8, 4, 4)

    def source_layer(src, count, k, high, j):
        if k == 0:
            return src[0:count, 3 if high else 0, j]
        if k == 1:
            return src[0:count, j, 7 if high else 0]
        z = 7 if high else 0
        return src[0:count, j, :, z, :]

    strides = (16, 4, 1)

    def pack(src, count, k, high):
        total = None
        last = packed_slots[k] - 1
        for j in range(packed_slots[k]):
            v = source_layer(src, count, k, high, j)
            v = roll(v, strides[k] * (j - (last if high else 0)), 2)
            total = v if total is None else jnp.where(slot_of[k] == j, v, total)
        return total

    def unpack(w, k, high, j):
        last = packed_slots[k] - 1
        v = roll(w, strides[k] * ((last if high else 0) - j), w.ndim - 1)
        return v

    def exchange(stage, src):
        count = 6 if stage == 0 else 5
        if stage == 0:
            for k in (1, 0, 2):
                for high in (0, 1):
                    send[stage, 2 * k + high, 0:count] = pack(src, count, k, high)
            pl.semaphore_wait(barrier, 8)
        copies = {}
        for k in (1, 0, 2):
            for high in (0, 1):
                mine = 2 * k + high
                if stage > 0:
                    send[stage, mine, 0:count] = pack(src, count, k, high)
                copy = pltpu.make_async_remote_copy(
                    src_ref=send.at[stage, mine, pl.ds(0, count)],
                    dst_ref=recv.at[stage, 2 * k + 1 - high, pl.ds(0, count)],
                    send_sem=ssem.at[stage, mine],
                    recv_sem=rsem.at[stage, 2 * k + 1 - high],
                    device_id=((above if high else below)[k],),
                    device_id_type=MESH,
                )
                copies[mine] = copy
                if k == 1:
                    copy.start()
                else:
                    pl.when(jnp.logical_not(at_end(k, high)))(copy.start)
        for k in (0, 2):
            for high in (0, 1):
                index = 2 * k + high

                @pl.when(at_end(k, high))
                def _():
                    for f in range(5):
                        recv[stage, index, f] = jnp.full((8, LANES), STREAM[f], f32)
                    if stage == 0:
                        recv[stage, index, 5] = send[stage, index, 5]
        return copies

    def at_end(k, high):
        return coord[k] == (extent[k] - 1 if high else 0)

    def shift_x(a):
        return jnp.concatenate([a[1:4], roll(a[0:1], -16, 2)], axis=0)

    def back_x(a):
        return jnp.concatenate([roll(a[3:4], 16, 2), a[0:3]], axis=0)

    def shift_y(a):
        return jnp.concatenate([a[1:8], roll(a[0:1], -4, 2)], axis=0)

    def back_y(a):
        return jnp.concatenate([roll(a[7:8], 4, 2), a[0:7]], axis=0)

    def shift_z(a):
        b = roll(a, -1, 1)
        return jnp.where(iz == 7, roll(b, -1, 2), b)

    def back_z(a):
        b = roll(a, 1, 1)
        return jnp.where(iz == 0, roll(b, 1, 2), b)

    slab = iota((4, 1, LANES), 0)
    mask_x = jnp.logical_not((slab == 3) & (block_x == 7))
    row = iota((8, 1, LANES), 0)
    mask_y = jnp.logical_not((row == 7) & (lane_by == 3))
    mask_z = jnp.logical_not((iz == 7) & ((lane_l & 3) == 3))

    def interior(src, want_lam):
        def pass_xz(y, carry):
            u = [src[f, :, y] for f in range(5)]
            a = u0[5, :, y]
            vel, p, c = prims(u)
            total = spread = None
            for k, ahead, back, mask in ((0, shift_x, back_x, mask_x), (2, shift_z, back_z, mask_z)):
                speed = jnp.abs(vel[k]) + c
                w, s = face(u, vel[k], p, speed, a,
                            [ahead(q) for q in u], ahead(vel[k]), ahead(p), ahead(speed), ahead(a),
                            k, mask)
                diff = [q - back(q) for q in w]
                total = diff if total is None else [t + d for t, d in zip(total, diff)]
                if want_lam:
                    both = s + back(s)
                    spread = both if spread is None else spread + both
            for f in range(5):
                res[f, :, y] = total[f]
            if want_lam:
                lam[:, y] = spread
            return carry

        lax.fori_loop(0, 8, pass_xz, 0, unroll=True)

        def pass_y(x, carry):
            u = [src[f, x] for f in range(5)]
            a = u0[5, x]
            vel, p, c = prims(u)
            speed = jnp.abs(vel[1]) + c
            w, s = face(u, vel[1], p, speed, a,
                        [shift_y(q) for q in u], shift_y(vel[1]), shift_y(p), shift_y(speed), shift_y(a),
                        1, mask_y)
            for f in range(5):
                res[f, x] = res[f, x] + (w[f] - back_y(w[f]))
            if want_lam:
                lam[x] = lam[x] + (s + back_y(s))
            return carry

        lax.fori_loop(0, 4, pass_y, 0, unroll=True)

    def boundary(stage, copies, want_lam):
        for k in (0, 2, 1):
            for high in (0, 1):
                if k == 1:
                    copies[2 * k + high].wait()
                else:
                    pl.when(jnp.logical_not(at_end(k, high)))(copies[2 * k + high].wait_send)
                    pl.when(jnp.logical_not(at_end(k, 1 - high)))(copies[2 * k + high].wait_recv)
        for k in range(3):
            for high in (0, 1):
                index = 2 * k + high
                own_u = [send[stage, index, f] for f in range(5)]
                own_a = send[0, index, 5]
                other_u = [recv[stage, index, f] for f in range(5)]
                other_a = recv[0, index, 5]
                if high:
                    w, s = face_from(own_u, own_a, other_u, other_a, k)
                    sign = 1.0
                else:
                    w, s = face_from(other_u, other_a, own_u, own_a, k)
                    sign = -1.0
                edge = packed_slots[k] - 1 if high else 0
                values = jnp.stack([sign * q for q in w] + ([s] if want_lam else []), axis=0)
                here = slot_of[k] == edge
                for j in range(packed_slots[k]):
                    add = jnp.where(here, unpack(values, k, high, j), 0.0)
                    if k == 0:
                        at = (3 if high else 0, j)
                    elif k == 1:
                        at = (j, 7 if high else 0)
                    else:
                        at = (j, slice(None), 7 if high else 0, slice(None))
                    where5 = (slice(0, 5),) + at
                    res[where5] = res[where5] + add[0:5]
                    if want_lam:
                        lam[at] = lam[at] + add[5]

    def box_x(a):
        up = jnp.where(ixhi == 0, roll(a[0:1], -16, 2), 0.0)
        down = jnp.where(ixhi == 1, roll(a[3:4], 16, 2), 0.0)
        return a + jnp.concatenate([a[1:4], up], axis=0) + jnp.concatenate([down, a[0:3]], axis=0)

    def box_y(a):
        zero = jnp.zeros_like(a[0:1])
        return a + jnp.concatenate([a[1:8], zero], axis=0) + jnp.concatenate([zero, a[0:7]], axis=0)

    def box_z(a):
        return a + jnp.where(iz == 7, 0.0, roll(a, -1, 1)) + jnp.where(iz == 0, 0.0, roll(a, 1, 1))

    def box_of_frac():
        def first(y, carry):
            box[0, :, y] = box_z(box_x(u0[5, :, y]))
            return carry
        lax.fori_loop(0, 8, first, 0, unroll=True)

        def second(x, carry):
            gain[x] = (1.0 - u0[5, x]) / box_y(box[0, x])
            return carry
        lax.fori_loop(0, 4, second, 0, unroll=True)

    def update(factor):
        def first(y, carry):
            share = u0[5, :, y] * (-CFL_NUMBER / lam[:, y])
            for f in range(5):
                d = share * res[f, :, y]
                res[f, :, y] = d
                box[f, :, y] = box_z(box_x(d))
            return carry
        lax.fori_loop(0, 8, first, 0, unroll=True)

        def second(x, carry):
            g = gain[x]
            for f in range(5):
                u1[f, x] = u0[f, x] + factor * (res[f, x] + g * box_y(box[f, x]))
            return carry
        lax.fori_loop(0, 4, second, 0, unroll=True)

    copies0 = exchange(0, u0)
    box_of_frac()
    interior(u0, True)
    boundary(0, copies0, True)
    update(FIRST_SECTION)

    copies1 = exchange(1, u1)
    interior(u1, True)
    boundary(1, copies1, True)
    update(1.0)

    copies2 = exchange(2, u1)

    coarse_count = brick // 8
    slot = par_lane >> 3
    slots = iota((coarse_count, LANES), 0)
    kept = jnp.where(slot == me * coarse_count + slots, 1.0, 0.0)
    sent = jnp.where(slot == nxt * coarse_count + slots, 1.0, 0.0)
    some_sent = jnp.max(sent, axis=1, keepdims=True)
    sent_before = jnp.sum(jnp.where(slots < slot - nxt * coarse_count, some_sent, 0.0),
                          axis=0, keepdims=True).astype(i32)
    goes = jnp.max(sent, axis=0, keepdims=True) > 0.5
    missing = 1.0 - jnp.max(kept, axis=1, keepdims=True)
    sq_row = iota((coarse_count, coarse_count), 0)
    sq_col = iota((coarse_count, coarse_count), 1)
    missing_row = jnp.sum(jnp.where(sq_row == sq_col, missing, 0.0), axis=0, keepdims=True)
    missing_before = jnp.sum(jnp.where(sq_col < sq_row, missing_row, 0.0),
                             axis=1, keepdims=True).astype(i32)
    r = iota((48, LANES), 0)
    ln = iota((48, LANES), 1)
    tile = (ln >> 4) & 3
    own_row = jnp.where((tile == (r >> 3)) & (slot == me * coarse_count + (r & 7)), 1.0, 0.0)
    sent_row = jnp.where((tile == ((r - 32) >> 2)) & (sent_before == (r & 3)) & goes, 1.0, 0.0)
    pick = jnp.where(r < 32, own_row, sent_row).astype(bf16)
    pick2 = jnp.concatenate([pick, pick], axis=1)
    lane_oy, lane_oz = (lane >> 2) & 1, lane & 1
    sub = iota((1, 8, LANES), 1)
    same_oz = (sub >> 2) == lane_oz

    def sums(x):
        g = x.reshape(2, 2, 4, 2, 8, LANES)
        s = (g[:, 0, :, 0] + g[:, 0, :, 1]) + (g[:, 1, :, 0] + g[:, 1, :, 1])
        s = s.reshape(8, 8, LANES)
        return s + roll(s, -1, 1)

    def coarse_rows(s):
        t = s
        for j in range(1, 4):
            t = jnp.where(sub == j, roll(s, -j, 1), t)
        t = jnp.where(sub >= 4, roll(t, 4, 1), t)
        t = jnp.where(same_oz, t, 0.0)
        both = [jnp.where(lane_oy == oy, t, 0.0) for oy in range(2)]
        return jnp.concatenate([both[0][0:4], both[1][0:4], both[0][4:8], both[1][4:8]],
                               axis=0).reshape(LANES, LANES)

    def coarse(group, values, out):
        z = jnp.concatenate([coarse_rows(s) for s in values], axis=0)
        hi, mid, _ = pieces(z)
        placed = dot(pick2, jnp.concatenate([hi, mid], axis=1), ((1,), (1,)))
        for f in range(5):
            block = placed[:, f * LANES:(f + 1) * LANES]
            csend[group, f] = block[32:48]
            for t in range(4):
                out[f, :, t * LANES:(t + 1) * LANES] = block[8 * t:8 * t + 8]

    def coarse_copy(group):
        copy = pltpu.make_async_remote_copy(
            src_ref=csend.at[group], dst_ref=crecv.at[group],
            send_sem=cssem.at[group], recv_sem=crsem.at[group],
            device_id=(nxt,), device_id_type=MESH)
        copy.start()
        return copy

    def coarse_finish(group, copy, out):
        copy.wait()
        for f in range(5):
            for t in range(4):
                at = (f, slice(None), slice(t * LANES, (t + 1) * LANES))
                arrived = crecv[group, f, 4 * t:4 * t + 4]
                total = out[at]
                for rank in range(4):
                    here = (missing > 0.5) & (missing_before == rank)
                    total = jnp.where(here, arrived[rank:rank + 1], total)
                out[at] = total

    inv = 1.0 / sums(u0[5])
    coarse(0, [sums(u0[5] * u1[f]) * inv for f in range(5)], cs_ref)
    state_copy = coarse_copy(0)

    interior(u1, False)

    boundary(2, copies2, False)
    coarse(1, [sums(res[f]) for f in range(5)], cr_ref)
    residual_copy = coarse_copy(1)

    perm_wide = jnp.concatenate([perm, perm], axis=1)
    for f in range(5):
        hi, mid, _ = pieces(u1[f].reshape(256, LANES))
        back = dot(perm_wide, jnp.concatenate([hi, mid], axis=1), ((1,), (1,)))
        fine_ref[f, :, 0:256] = back[0:brick]
        fine_ref[f, :, 256:512] = back[brick:2 * brick]

    coarse_finish(0, state_copy, cs_ref)
    coarse_finish(1, residual_copy, cr_ref)


def write_out(*refs):
    sources, targets, sem = refs[:3], refs[3:6], refs[6]
    copies = [pltpu.make_async_copy(sources[i], targets[i], sem.at[i]) for i in range(3)]
    for copy in copies:
        copy.start()
    for copy in copies:
        copy.wait()


def local(n, state, volume, neighbour, parent):
    brick = state.shape[1]
    grid = (4, 8, 8, LANES)
    vmem = pl.BlockSpec(memory_space=pltpu.VMEM)
    hbm = pl.BlockSpec(memory_space=pltpu.HBM)
    coarse_shape = jax.ShapeDtypeStruct((5, brick // 8, BE ** 3), f32)
    shapes = (jax.ShapeDtypeStruct(state.shape, f32), coarse_shape, coarse_shape)
    held = pl.pallas_call(
        functools.partial(kernel, n),
        out_shape=tuple(pltpu.VMEM(one.shape, one.dtype) for one in shapes),
        in_specs=[hbm, vmem, vmem, hbm],
        out_specs=(vmem,) * 3,
        scratch_shapes=[
            pltpu.VMEM(volume.shape, i32),
            pltpu.VMEM(state.shape, f32),
            pltpu.SemaphoreType.DMA((6,)),
            pltpu.VMEM((6,) + grid, f32),
            pltpu.VMEM((5,) + grid, f32),
            pltpu.VMEM((5,) + grid, f32),
            pltpu.VMEM(grid, f32),
            pltpu.VMEM((5,) + grid, f32),
            pltpu.VMEM(grid, f32),
            pltpu.VMEM((3, 6, 6, 8, LANES), f32),
            pltpu.VMEM((3, 6, 6, 8, LANES), f32),
            pltpu.VMEM((2, 5, 16, LANES), f32),
            pltpu.VMEM((2, 5, 16, LANES), f32),
            pltpu.SemaphoreType.DMA((3, 6)),
            pltpu.SemaphoreType.DMA((3, 6)),
            pltpu.SemaphoreType.DMA((2,)),
            pltpu.SemaphoreType.DMA((2,)),
        ],
        compiler_params=pltpu.CompilerParams(
            collective_id=0, has_side_effects=True, vmem_limit_bytes=60 * 1024 * 1024),
    )(volume, neighbour.T, parent.reshape(1, brick), state)
    return pl.pallas_call(
        write_out,
        out_shape=shapes,
        in_specs=[vmem] * 3,
        out_specs=(hbm,) * 3,
        scratch_shapes=[pltpu.SemaphoreType.DMA((3,))],
        compiler_params=pltpu.CompilerParams(vmem_limit_bytes=4 * 1024 * 1024),
    )(*held)


def solution(mesh):
    in_specs = (P(None, "sfc", None), P("sfc", None), P("sfc", None), P("sfc"))
    out_specs = (P(None, "sfc", None), P(None, "sfc", None), P(None, "sfc", None))
    return jax.shard_map(functools.partial(local, mesh.shape["sfc"]), mesh=mesh,
                         in_specs=in_specs, out_specs=out_specs, check_vma=False)
```

```python
import functools

import jax
import jax.numpy as jnp
from jax import lax
from jax.experimental import pallas as pl
from jax.experimental.pallas import tpu as pltpu
from jax.sharding import PartitionSpec as P

BE = 8
CUBE = 4
LANES = 128
CFL_NUMBER = 0.25
FIRST_SECTION = 0.5
STREAM = (1.0, 0.5, 0.0, 0.0, 1.0 / (1.4 * (1.4 - 1.0)) + 0.125)
f32 = jnp.float32
bf16 = jnp.bfloat16
i32 = jnp.int32
MESH = pl.DeviceIdType.MESH


def iota(shape, dim):
    return lax.broadcasted_iota(i32, shape, dim)


def pieces(x):
    hi = x.astype(bf16)
    rest = x - hi.astype(f32)
    mid = rest.astype(bf16)
    low = (rest - mid.astype(f32)).astype(bf16)
    return hi, mid, low


def dot(a, b, dims):
    return lax.dot_general(a, b, (dims, ((), ())), preferred_element_type=f32)


def prims(u):
    inv = 1.0 / u[0]
    vel = [u[1] * inv, u[2] * inv, u[3] * inv]
    kinetic = 0.5 * (u[1] * vel[0] + u[2] * vel[1] + u[3] * vel[2])
    pressure = 0.4 * (u[4] - kinetic)
    sound = jnp.sqrt(1.4 * pressure * inv)
    return vel, pressure, sound


def flux(u, v, p, k):
    out = [u[1 + k]]
    for j in range(3):
        m = u[1 + j] * v
        out.append(m + p if j == k else m)
    out.append((u[4] + p) * v)
    return out


def face(ul, vl, pl_, sl, al, ur, vr, pr, sr, ar, k, mask):
    s = jnp.maximum(sl, sr)
    a = jnp.minimum(al, ar)
    if mask is not None:
        a = jnp.where(mask, a, 0.0)
    half = 0.5 * a
    fl = flux(ul, vl, pl_, k)
    fr = flux(ur, vr, pr, k)
    w = [half * ((fl[i] + fr[i]) - s * (ur[i] - ul[i])) for i in range(5)]
    return w, a * s


def face_from(ul, al, ur, ar, k, mask=None):
    vl, pl_, cl = prims(ul)
    vr, pr, cr = prims(ur)
    return face(ul, vl[k], pl_, jnp.abs(vl[k]) + cl, al,
                ur, vr[k], pr, jnp.abs(vr[k]) + cr, ar, k, mask)


def roll(x, shift, axis):
    size = x.shape[axis]
    shift = shift % size
    return x if shift == 0 else pltpu.roll(x, shift, axis)


def kernel(n, vol_hbm, nb_ref, par_ref, x_hbm,
           fine_ref, cs_ref, cr_ref,
           vol_ref, x_ref, in_sem, u0, u1, res, lam, box, gain, send, recv, csend, crecv,
           ssem, rsem, cssem, crsem):
    me = lax.axis_index("sfc")
    bits = n.bit_length() - 1
    brick = x_ref.shape[1]
    cells = BE ** 3

    loads = [pltpu.make_async_copy(vol_hbm, vol_ref, in_sem.at[5])]
    for f in range(5):
        loads.append(pltpu.make_async_copy(x_hbm.at[f], x_ref.at[f], in_sem.at[f]))
    for load in loads:
        load.start()

    coord, extent = [], []
    for k in range(3):
        value, size = 0, 1
        for i in range(bits):
            if i % 3 == k:
                value = value + (me // (1 << i)) % 2 * size
                size *= 2
        coord.append(value)
        extent.append(size)

    def device_at(axis, value):
        out = 0
        for i in range(bits):
            k = i % 3
            source = value if k == axis else coord[k]
            out = out + (source // (1 << (i // 3))) % 2 * (1 << i)
        return out

    below = [device_at(k, (coord[k] + extent[k] - 1) % extent[k]) for k in range(3)]
    above = [device_at(k, (coord[k] + 1) % extent[k]) for k in range(3)]
    nxt, prev = (me + 1) % n, (me + n - 1) % n

    barrier = pltpu.get_barrier_semaphore()
    for target in below + above + [nxt, prev]:
        pl.semaphore_signal(barrier, inc=1, device_id=(target,), device_id_type=MESH)

    nb = nb_ref[...]
    par = par_ref[...]
    octant = par & 7
    remote = jnp.where((nb < 0) | (lax.div(jnp.maximum(nb, 0), brick) != me), 1, 0)

    def position(axis, parity):
        low = remote[2 * axis:2 * axis + 1]
        high = remote[2 * axis + 1:2 * axis + 2]
        return jnp.where(parity == 0, 2 - 2 * low, 1 + 2 * high)

    bx = position(0, octant >> 2)
    by = position(1, (octant >> 1) & 1)
    bz = position(2, octant & 1)
    eye = iota((brick, brick), 0) == iota((brick, brick), 1)

    def column(r):
        return jnp.sum(jnp.where(eye, r.astype(f32), 0.0), axis=1, keepdims=True)

    par_col = column(par)
    lane0 = column(bx * 32 + by * 4 + bz).astype(i32)
    lane2 = jnp.concatenate([lane0, lane0 + 16], axis=0)
    hot = iota((2 * brick, LANES), 1) == lane2
    perm = jnp.where(hot, 1.0, 0.0).astype(bf16)
    par_lane = jnp.sum(jnp.where(hot, jnp.concatenate([par_col, par_col], axis=0), 0.0),
                       axis=0, keepdims=True).astype(i32)

    def to_grid(x):
        both = jnp.concatenate([x[:, :cells // 2], x[:, cells // 2:]], axis=0)
        return both

    perm2 = jnp.concatenate([perm, perm], axis=0)
    loads[0].wait()
    volume = (to_grid(vol_ref[...]).astype(f32) * 0.125).astype(bf16)
    u0[5] = dot(volume, perm, ((0,), (0,))).reshape(4, 8, 8, LANES)
    for f in range(5):
        loads[1 + f].wait()
        hi, mid, low = pieces(to_grid(x_ref[f]))
        total = (dot(jnp.concatenate([hi, mid], axis=0), perm2, ((0,), (0,)))
                 + dot(low, perm, ((0,), (0,))))
        u0[f] = total.reshape(4, 8, 8, LANES)

    lane = iota((1, 1, LANES), 2)
    block_x, lane_by, lane_bz = lane >> 4, (lane >> 2) & 3, lane & 3
    ixhi = (lane >> 4) & 1
    iz = iota((1, 8, LANES), 1)
    lane_l = iota((1, 8, LANES), 2)

    slot_of = (block_x, lane_by, lane_bz)
    packed_slots = (8, 4, 4)

    def source_layer(src, count, k, high, j):
        if k == 0:
            return src[0:count, 3 if high else 0, j]
        if k == 1:
            return src[0:count, j, 7 if high else 0]
        z = 7 if high else 0
        return src[0:count, j, :, z, :]

    strides = (16, 4, 1)

    def pack(src, count, k, high):
        total = None
        last = packed_slots[k] - 1
        for j in range(packed_slots[k]):
            v = source_layer(src, count, k, high, j)
            v = roll(v, strides[k] * (j - (last if high else 0)), 2)
            total = v if total is None else jnp.where(slot_of[k] == j, v, total)
        return total

    def unpack(w, k, high, j):
        last = packed_slots[k] - 1
        v = roll(w, strides[k] * ((last if high else 0) - j), w.ndim - 1)
        return v

    def exchange(stage, src):
        count = 6 if stage == 0 else 5
        if stage == 0:
            for k in (1, 0, 2):
                for high in (0, 1):
                    send[stage, 2 * k + high, 0:count] = pack(src, count, k, high)
            pl.semaphore_wait(barrier, 8)
        copies = {}
        for k in (1, 0, 2):
            for high in (0, 1):
                mine = 2 * k + high
                if stage > 0:
                    send[stage, mine, 0:count] = pack(src, count, k, high)
                copy = pltpu.make_async_remote_copy(
                    src_ref=send.at[stage, mine, pl.ds(0, count)],
                    dst_ref=recv.at[stage, 2 * k + 1 - high, pl.ds(0, count)],
                    send_sem=ssem.at[stage, mine],
                    recv_sem=rsem.at[stage, 2 * k + 1 - high],
                    device_id=((above if high else below)[k],),
                    device_id_type=MESH,
                )
                copies[mine] = copy
                if k == 1:
                    copy.start()
                else:
                    pl.when(jnp.logical_not(at_end(k, high)))(copy.start)
        for k in (0, 2):
            for high in (0, 1):
                index = 2 * k + high

                @pl.when(at_end(k, high))
                def _():
                    for f in range(5):
                        recv[stage, index, f] = jnp.full((8, LANES), STREAM[f], f32)
                    if stage == 0:
                        recv[stage, index, 5] = send[stage, index, 5]
        return copies

    def at_end(k, high):
        return coord[k] == (extent[k] - 1 if high else 0)

    def shift_x(a):
        return jnp.concatenate([a[1:4], roll(a[0:1], -16, 2)], axis=0)

    def back_x(a):
        return jnp.concatenate([roll(a[3:4], 16, 2), a[0:3]], axis=0)

    def shift_y(a):
        return jnp.concatenate([a[1:8], roll(a[0:1], -4, 2)], axis=0)

    def back_y(a):
        return jnp.concatenate([roll(a[7:8], 4, 2), a[0:7]], axis=0)

    def shift_z(a):
        b = roll(a, -1, 1)
        return jnp.where(iz == 7, roll(b, -1, 2), b)

    def back_z(a):
        b = roll(a, 1, 1)
        return jnp.where(iz == 0, roll(b, 1, 2), b)

    slab = iota((4, 1, LANES), 0)
    mask_x = jnp.logical_not((slab == 3) & (block_x == 7))
    row = iota((8, 1, LANES), 0)
    mask_y = jnp.logical_not((row == 7) & (lane_by == 3))
    mask_z = jnp.logical_not((iz == 7) & ((lane_l & 3) == 3))

    def interior(src, want_lam):
        def pass_xz(y, carry):
            u = [src[f, :, y] for f in range(5)]
            a = u0[5, :, y]
            vel, p, c = prims(u)
            total = spread = None
            for k, ahead, back, mask in ((0, shift_x, back_x, mask_x), (2, shift_z, back_z, mask_z)):
                speed = jnp.abs(vel[k]) + c
                w, s = face(u, vel[k], p, speed, a,
                            [ahead(q) for q in u], ahead(vel[k]), ahead(p), ahead(speed), ahead(a),
                            k, mask)
                diff = [q - back(q) for q in w]
                total = diff if total is None else [t + d for t, d in zip(total, diff)]
                if want_lam:
                    both = s + back(s)
                    spread = both if spread is None else spread + both
            for f in range(5):
                res[f, :, y] = total[f]
            if want_lam:
                lam[:, y] = spread
            return carry

        lax.fori_loop(0, 8, pass_xz, 0, unroll=True)

        def pass_y(x, carry):
            u = [src[f, x] for f in range(5)]
            a = u0[5, x]
            vel, p, c = prims(u)
            speed = jnp.abs(vel[1]) + c
            w, s = face(u, vel[1], p, speed, a,
                        [shift_y(q) for q in u], shift_y(vel[1]), shift_y(p), shift_y(speed), shift_y(a),
                        1, mask_y)
            for f in range(5):
                res[f, x] = res[f, x] + (w[f] - back_y(w[f]))
            if want_lam:
                lam[x] = lam[x] + (s + back_y(s))
            return carry

        lax.fori_loop(0, 4, pass_y, 0, unroll=True)

    def boundary(stage, copies, want_lam):
        for k in (0, 2, 1):
            for high in (0, 1):
                if k == 1:
                    copies[2 * k + high].wait()
                else:
                    pl.when(jnp.logical_not(at_end(k, high)))(copies[2 * k + high].wait_send)
                    pl.when(jnp.logical_not(at_end(k, 1 - high)))(copies[2 * k + high].wait_recv)
        for k in range(3):
            for high in (0, 1):
                index = 2 * k + high
                own_u = [send[stage, index, f] for f in range(5)]
                own_a = send[0, index, 5]
                other_u = [recv[stage, index, f] for f in range(5)]
                other_a = recv[0, index, 5]
                if high:
                    w, s = face_from(own_u, own_a, other_u, other_a, k)
                    sign = 1.0
                else:
                    w, s = face_from(other_u, other_a, own_u, own_a, k)
                    sign = -1.0
                edge = packed_slots[k] - 1 if high else 0
                values = jnp.stack([sign * q for q in w] + ([s] if want_lam else []), axis=0)
                here = slot_of[k] == edge
                for j in range(packed_slots[k]):
                    add = jnp.where(here, unpack(values, k, high, j), 0.0)
                    if k == 0:
                        at = (3 if high else 0, j)
                    elif k == 1:
                        at = (j, 7 if high else 0)
                    else:
                        at = (j, slice(None), 7 if high else 0, slice(None))
                    where5 = (slice(0, 5),) + at
                    res[where5] = res[where5] + add[0:5]
                    if want_lam:
                        lam[at] = lam[at] + add[5]

    def box_x(a):
        up = jnp.where(ixhi == 0, roll(a[0:1], -16, 2), 0.0)
        down = jnp.where(ixhi == 1, roll(a[3:4], 16, 2), 0.0)
        return a + jnp.concatenate([a[1:4], up], axis=0) + jnp.concatenate([down, a[0:3]], axis=0)

    def box_y(a):
        zero = jnp.zeros_like(a[0:1])
        return a + jnp.concatenate([a[1:8], zero], axis=0) + jnp.concatenate([zero, a[0:7]], axis=0)

    def box_z(a):
        return a + jnp.where(iz == 7, 0.0, roll(a, -1, 1)) + jnp.where(iz == 0, 0.0, roll(a, 1, 1))

    def box_of_frac():
        def first(y, carry):
            box[0, :, y] = box_z(box_x(u0[5, :, y]))
            return carry
        lax.fori_loop(0, 8, first, 0, unroll=True)

        def second(x, carry):
            gain[x] = (1.0 - u0[5, x]) / box_y(box[0, x])
            return carry
        lax.fori_loop(0, 4, second, 0, unroll=True)

    def update(factor):
        def first(y, carry):
            share = u0[5, :, y] * (-CFL_NUMBER / lam[:, y])
            for f in range(5):
                d = share * res[f, :, y]
                res[f, :, y] = d
                box[f, :, y] = box_z(box_x(d))
            return carry
        lax.fori_loop(0, 8, first, 0, unroll=True)

        def second(x, carry):
            g = gain[x]
            for f in range(5):
                u1[f, x] = u0[f, x] + factor * (res[f, x] + g * box_y(box[f, x]))
            return carry
        lax.fori_loop(0, 4, second, 0, unroll=True)

    copies0 = exchange(0, u0)
    box_of_frac()
    interior(u0, True)
    boundary(0, copies0, True)
    update(FIRST_SECTION)

    copies1 = exchange(1, u1)
    interior(u1, True)
    boundary(1, copies1, True)
    update(1.0)

    copies2 = exchange(2, u1)

    coarse_count = brick // 8
    slot = par_lane >> 3
    slots = iota((coarse_count, LANES), 0)
    kept = jnp.where(slot == me * coarse_count + slots, 1.0, 0.0)
    sent = jnp.where(slot == nxt * coarse_count + slots, 1.0, 0.0)
    some_sent = jnp.max(sent, axis=1, keepdims=True)
    sent_before = jnp.sum(jnp.where(slots < slot - nxt * coarse_count, some_sent, 0.0),
                          axis=0, keepdims=True).astype(i32)
    goes = jnp.max(sent, axis=0, keepdims=True) > 0.5
    missing = 1.0 - jnp.max(kept, axis=1, keepdims=True)
    sq_row = iota((coarse_count, coarse_count), 0)
    sq_col = iota((coarse_count, coarse_count), 1)
    missing_row = jnp.sum(jnp.where(sq_row == sq_col, missing, 0.0), axis=0, keepdims=True)
    missing_before = jnp.sum(jnp.where(sq_col < sq_row, missing_row, 0.0),
                             axis=1, keepdims=True).astype(i32)
    r = iota((48, LANES), 0)
    ln = iota((48, LANES), 1)
    tile = (ln >> 4) & 3
    own_row = jnp.where((tile == (r >> 3)) & (slot == me * coarse_count + (r & 7)), 1.0, 0.0)
    sent_row = jnp.where((tile == ((r - 32) >> 2)) & (sent_before == (r & 3)) & goes, 1.0, 0.0)
    pick = jnp.where(r < 32, own_row, sent_row).astype(bf16)
    pick2 = jnp.concatenate([pick, pick], axis=1)
    lane_oy, lane_oz = (lane >> 2) & 1, lane & 1
    sub = iota((1, 8, LANES), 1)
    same_oz = (sub >> 2) == lane_oz

    def sums(x):
        g = x.reshape(2, 2, 4, 2, 8, LANES)
        s = (g[:, 0, :, 0] + g[:, 0, :, 1]) + (g[:, 1, :, 0] + g[:, 1, :, 1])
        s = s.reshape(8, 8, LANES)
        return s + roll(s, -1, 1)

    def coarse_rows(s):
        t = s
        for j in range(1, 4):
            t = jnp.where(sub == j, roll(s, -j, 1), t)
        t = jnp.where(sub >= 4, roll(t, 4, 1), t)
        t = jnp.where(same_oz, t, 0.0)
        both = [jnp.where(lane_oy == oy, t, 0.0) for oy in range(2)]
        return jnp.concatenate([both[0][0:4], both[1][0:4], both[0][4:8], both[1][4:8]],
                               axis=0).reshape(LANES, LANES)

    def coarse(group, values, out):
        z = jnp.concatenate([coarse_rows(s) for s in values], axis=0)
        hi, mid, _ = pieces(z)
        placed = dot(pick2, jnp.concatenate([hi, mid], axis=1), ((1,), (1,)))
        for f in range(5):
            block = placed[:, f * LANES:(f + 1) * LANES]
            csend[group, f] = block[32:48]
            for t in range(4):
                out[f, :, t * LANES:(t + 1) * LANES] = block[8 * t:8 * t + 8]

    def coarse_copy(group):
        copy = pltpu.make_async_remote_copy(
            src_ref=csend.at[group], dst_ref=crecv.at[group],
            send_sem=cssem.at[group], recv_sem=crsem.at[group],
            device_id=(nxt,), device_id_type=MESH)
        copy.start()
        return copy

    def coarse_finish(group, copy, out):
        copy.wait()
        for f in range(5):
            for t in range(4):
                at = (f, slice(None), slice(t * LANES, (t + 1) * LANES))
                arrived = crecv[group, f, 4 * t:4 * t + 4]
                total = out[at]
                for rank in range(4):
                    here = (missing > 0.5) & (missing_before == rank)
                    total = jnp.where(here, arrived[rank:rank + 1], total)
                out[at] = total

    interior(u1, False)

    inv = 1.0 / sums(u0[5])
    coarse(0, [sums(u0[5] * u1[f]) * inv for f in range(5)], cs_ref)
    state_copy = coarse_copy(0)

    boundary(2, copies2, False)
    coarse(1, [sums(res[f]) for f in range(5)], cr_ref)
    residual_copy = coarse_copy(1)

    perm_wide = jnp.concatenate([perm, perm], axis=1)
    for f in range(5):
        hi, mid, _ = pieces(u1[f].reshape(256, LANES))
        back = dot(perm_wide, jnp.concatenate([hi, mid], axis=1), ((1,), (1,)))
        fine_ref[f, :, 0:256] = back[0:brick]
        fine_ref[f, :, 256:512] = back[brick:2 * brick]

    coarse_finish(0, state_copy, cs_ref)
    coarse_finish(1, residual_copy, cr_ref)


def write_out(*refs):
    sources, targets, sem = refs[:3], refs[3:6], refs[6]
    copies = [pltpu.make_async_copy(sources[i], targets[i], sem.at[i]) for i in range(3)]
    for copy in copies:
        copy.start()
    for copy in copies:
        copy.wait()


def local(n, state, volume, neighbour, parent):
    brick = state.shape[1]
    grid = (4, 8, 8, LANES)
    vmem = pl.BlockSpec(memory_space=pltpu.VMEM)
    hbm = pl.BlockSpec(memory_space=pltpu.HBM)
    coarse_shape = jax.ShapeDtypeStruct((5, brick // 8, BE ** 3), f32)
    shapes = (jax.ShapeDtypeStruct(state.shape, f32), coarse_shape, coarse_shape)
    held = pl.pallas_call(
        functools.partial(kernel, n),
        out_shape=tuple(pltpu.VMEM(one.shape, one.dtype) for one in shapes),
        in_specs=[hbm, vmem, vmem, hbm],
        out_specs=(vmem,) * 3,
        scratch_shapes=[
            pltpu.VMEM(volume.shape, i32),
            pltpu.VMEM(state.shape, f32),
            pltpu.SemaphoreType.DMA((6,)),
            pltpu.VMEM((6,) + grid, f32),
            pltpu.VMEM((5,) + grid, f32),
            pltpu.VMEM((5,) + grid, f32),
            pltpu.VMEM(grid, f32),
            pltpu.VMEM((5,) + grid, f32),
            pltpu.VMEM(grid, f32),
            pltpu.VMEM((3, 6, 6, 8, LANES), f32),
            pltpu.VMEM((3, 6, 6, 8, LANES), f32),
            pltpu.VMEM((2, 5, 16, LANES), f32),
            pltpu.VMEM((2, 5, 16, LANES), f32),
            pltpu.SemaphoreType.DMA((3, 6)),
            pltpu.SemaphoreType.DMA((3, 6)),
            pltpu.SemaphoreType.DMA((2,)),
            pltpu.SemaphoreType.DMA((2,)),
        ],
        compiler_params=pltpu.CompilerParams(
            collective_id=0, has_side_effects=True, vmem_limit_bytes=60 * 1024 * 1024),
    )(volume, neighbour.T, parent.reshape(1, brick), state)
    return pl.pallas_call(
        write_out,
        out_shape=shapes,
        in_specs=[vmem] * 3,
        out_specs=(hbm,) * 3,
        scratch_shapes=[pltpu.SemaphoreType.DMA((3,))],
        compiler_params=pltpu.CompilerParams(vmem_limit_bytes=4 * 1024 * 1024),
    )(*held)


def solution(mesh):
    in_specs = (P(None, "sfc", None), P("sfc", None), P("sfc", None), P("sfc"))
    out_specs = (P(None, "sfc", None), P(None, "sfc", None), P(None, "sfc", None))
    return jax.shard_map(functools.partial(local, mesh.shape["sfc"]), mesh=mesh,
                         in_specs=in_specs, out_specs=out_specs, check_vma=False)
```
